32 devices in a mesh: beam: 8 (over y, x, core), expert: 4 (over z).
Axes of the slice: x: 2, y: 2, z: 4, core: 2. Of those that a mesh axis runs over, the one named last changes fastest.
Arguments:
- layer_input: bfloat16 [2, 128, 2048], P(None, 'beam'), may hold values from -6 to 6
- queries: bfloat16 [2, 128, 2048], P(None, 'beam', 'expert'), may hold values from -24 to 24
- new_keys: bfloat16 [2, 128, 2048], P(None, 'beam', 'expert'), may hold values from -4.5 to 4.5
- new_values: bfloat16 [2, 128, 2048], P(None, 'beam', 'expert'), may hold values from -6 to 6
- cache_keys: bfloat16 [128, 32, 2048], P('beam', None, 'expert'), may hold values from -4.5 to 4.5
- cache_values: bfloat16 [128, 32, 2048], P('beam', None, 'expert'), may hold values from -6 to 6
- parents: int32 [2, 128], replicated, may hold values from 0 to 3
- lengths: int32 [32], replicated, may hold values from 1 to 32, as said below
- out_weight: bfloat16 [2048, 2048], P('expert'), may hold values from -0.125 to 0.125
- norm_gain: float32 [2048], replicated, may hold values from 0.25 to 1.75
- expert_ids: int32 [2, 128, 2], P(None, 'beam'), may hold values from 0 to 31, all different within a row; in each aligned block of 16 rows (0 to 15, 16 to 31, ..., all dimensions but the last counted through in order) at most 2 rows name the same one
- gate_scores: float32 [2, 128, 2], P(None, 'beam'), may hold values from 0.1 to 1
- up_weight: bfloat16 [32, 2048, 8192], P('expert', None, 'beam'), may hold values from -0.125 to 0.125
- down_weight: bfloat16 [32, 8192, 2048], P('expert', 'beam'), may hold values from -0.09375 to 0.09375
Outputs:
- mixed: bfloat16 [2, 128, 2048], P(None, 'beam', 'expert')
The draws below stay inside these ranges and needn't reach their ends.
Inputs may be any that keep to these rules, and one draw needn't show every extreme that they name: `expert_ids`: among the 32 choices of each aligned block of 16 rows of one step, no expert appears more than 2 times, a bound that some block reaches; a row's choices differ. `lengths`: some sentence has all 32 positions valid.
All inputs are finite; a program needn't handle non-finite values.
Results may differ from the reference program's by a relative error of at most 0.012.
Values may be sent and summed in bfloat16 or wider, within the bound.
No kernel may reach another device: no remote copies, remote signals or barrier semaphores. Data moves between devices by JAX's collectives and lax.ppermute only.
A program may use at most 192 MiB of HBM per device.

```python
import math
import jax
import jax.numpy as jnp
import numpy as np
from jax import lax

D = 2048
HEADS = 16
HEAD_DIM = 128
EXPERTS = 32
FF = 8192
TOP = 2
CAP = 2
BEAM = 4
STEPS = 2
SLOT_SENT = 16
PAST = 32
SENT = 32
ROWS = 128
N_BEAM = 8


def draw_queries(key, part):
    key = jax.random.fold_in(key, 1)
    drawn = jnp.clip(jax.random.normal(key, (STEPS, BEAM * SENT, HEADS * HEAD_DIM), jnp.float32), -4.5, 4.5)
    return drawn.astype(jnp.bfloat16)


def draw_new_keys(key, part):
    key = jax.random.fold_in(key, 2)
    noise = jnp.clip(jax.random.normal(key, (STEPS, BEAM * SENT, HEADS * HEAD_DIM), jnp.float32), -4.5, 4.5)
    drawn = noise
    return drawn.astype(jnp.bfloat16)


def draw_cache_keys(key, part):
    key = jax.random.fold_in(key, 3)
    noise = jnp.clip(jax.random.normal(key, (BEAM * SENT, PAST, HEADS * HEAD_DIM), jnp.float32), -4.5, 4.5)
    drawn = noise
    return drawn.astype(jnp.bfloat16)


def draw_lengths(key, part):
    key = jax.random.fold_in(key, 4)
    drawn = jax.random.randint(key, (SENT,), 1, PAST + 1)
    full_place = jax.random.randint(jax.random.fold_in(key, 1), (), 0, SENT)
    drawn = drawn.at[full_place].set(PAST)
    drawn = drawn.at[(full_place + 1) % SENT].set(1)
    return drawn.astype(jnp.int32)


def place_ends(values, key, smallest, largest):
    shape = values.shape
    index_at = [jax.random.randint(jax.random.fold_in(key, axis), (), 0, shape[axis]) for axis in range(len(shape))]
    values = values.at[tuple(index_at)].set(smallest)
    longest = shape.index(max(shape))
    index_at[longest] = (index_at[longest] + 1) % shape[longest]
    return values.at[tuple(index_at)].set(largest)


def spiked(result, rng, source, target, shards_of, factor):
    def block_of(dim):
        return (jnp.arange(result.shape[dim]) // (result.shape[dim] // shards_of)).reshape((-1,) + (1,) * (result.ndim - 1 - dim))

    one_side = jax.random.permutation(rng, shards_of)[block_of(target)]
    far = (block_of(target) + shards_of // 2) % shards_of
    return jnp.where((block_of(source) == one_side) | (block_of(source) == far), factor * result, result)


def block_levels(stream_key, dims, split, smallest, top_value):
    factor_of = 1.0
    for dim, blocks in split:
        draws = jax.random.uniform(jax.random.fold_in(jax.random.fold_in(stream_key, 6), dim), (blocks,), jnp.float32, smallest / len(split), top_value / len(split))
        factor_of = factor_of * jnp.repeat(jnp.exp(draws), dims[dim] // blocks).reshape((-1,) + (1,) * (len(dims) - 1 - dim))
    return factor_of


def assign_block(key, own, number, rows, amount, top, most, slope):
    ranking = jax.random.permutation(key, amount)
    heavy_load, usual = shares(amount, rows * top, most, slope, True), shares(amount, rows * top, most, slope, False)
    places = jnp.arange(amount)

    def named(tallies, rotation):
        used = int((tallies > 0).sum())
        fixed = max(1, used // 4)
        moved = fixed + (places - fixed + rotation * (used - fixed)) % max(1, amount - fixed)
        return jnp.zeros((amount,), jnp.int32).at[ranking[jnp.where(places < fixed, places, moved)]].set(jnp.asarray(tallies, jnp.int32))

    tallies = jnp.where(number % 4 == 0, named(heavy_load, number // 4), named(usual, number - number // 4 - 1))
    mixed = jax.random.permutation(jax.random.fold_in(own, 3), amount)
    source_of, taker = mixed[0:amount // 2 * 2:2], mixed[1:amount // 2 * 2:2]
    slack = jnp.minimum(tallies[source_of] - 1, most - tallies[taker]) // 2
    slack = jnp.where((source_of == ranking[0]) | (taker == ranking[0]) | (tallies[taker] == 0), 0, jnp.maximum(slack, 0))
    moved = jax.random.randint(jax.random.fold_in(own, 4), (amount // 2,), 0, 1 << 20) % (slack + 1)
    tallies = tallies.at[source_of].add(-moved).at[taker].add(moved)
    items = jnp.searchsorted(jnp.cumsum(tallies), jnp.arange(rows * top), side="right").astype(jnp.int32)
    grid = items.reshape(top, rows).T
    grid = grid[jax.random.permutation(jax.random.fold_in(own, 1), rows)]
    rotation = jax.random.randint(jax.random.fold_in(own, 2), (rows, 1), 0, top)
    return jnp.take_along_axis(grid, (jnp.arange(top)[None, :] + rotation) % top, axis=1)


def shares(count, total, limit, lean, full):
    portions = [(1 << 20) // math.isqrt(rank ** lean) + 1 for rank in range(1, count + 1)]
    largest = limit if full else min(limit, max(-(-total // count), total * portions[0] // sum(portions)))
    least = 1 if total - largest >= count - 1 else 0
    holding, surplus = [largest] + [least] * (count - 1), total - largest - least * (count - 1)
    while surplus > 0:
        candidates = [i for i in range(1, count) if holding[i] < largest] or [i for i in range(1, count) if holding[i] < limit]
        pool, remaining = sum([portions[i] for i in candidates]), surplus
        for i in candidates:
            addition = min(limit - holding[i], max(1, remaining * portions[i] // pool), surplus)
            holding[i] = holding[i] + addition
            surplus = surplus - addition
    return np.array(holding)


def gaussian(key, dims, scale, bound, cuts=(), kind=jnp.bfloat16):
    result = scale * jax.random.normal(key, dims, jnp.float32)
    if cuts:
        result = result * block_levels(key, dims, cuts, -0.22, 0.18)
    return jnp.clip(result, -bound, bound).astype(kind)


def bell_draw_with(stream_key, shape, scale, limit, shards, heavy, kind=jnp.bfloat16):
    values = scale * jax.random.normal(stream_key, shape, jnp.float32)
    if shards:
        values = values * block_levels(stream_key, shape, shards, -0.22, 0.18)
    return jnp.clip(spiked(values, jax.random.fold_in(stream_key, 3), *heavy), -limit, limit).astype(kind)


def setup_inputs(seed: int = 0) -> dict:
    keys = jax.random.split(jax.random.key(seed), 15)
    layer_input = gaussian(keys[0], (STEPS, ROWS, D), 1.0, 6.0, ((1, 8),))
    queries = draw_queries(jax.random.fold_in(keys[14], 71), 0)
    new_keys = draw_new_keys(jax.random.fold_in(keys[14], 71), 0)
    new_values = gaussian(keys[3], (STEPS, ROWS, HEADS * HEAD_DIM), 1.0, 6.0, ((1, 8), (2, 4)))
    cache_keys = draw_cache_keys(jax.random.fold_in(keys[14], 71), 0)
    cache_values = gaussian(keys[5], (ROWS, PAST, HEADS * HEAD_DIM), 1.0, 6.0, ((0, 8), (2, 4)))
    parents = place_ends(jax.random.randint(keys[6], (STEPS, ROWS), 0, BEAM), jax.random.fold_in(keys[6], 1), 0, BEAM - 1).astype(jnp.int32)
    lengths = draw_lengths(jax.random.fold_in(keys[14], 71), 0)
    out_weight = gaussian(keys[8], (HEADS * HEAD_DIM, D), (HEADS * HEAD_DIM) ** -0.5, 0.125, ((0, 4),))
    norm_gain = jnp.clip(1.0 + 0.15 * jax.random.normal(keys[9], (D,), jnp.float32), 0.25, 1.75)
    expert_ids_keys = jax.random.split(jax.random.fold_in(keys[10], 1), STEPS * ROWS // SLOT_SENT)
    expert_ids_turns = jax.random.permutation(jax.random.fold_in(keys[10], 3), STEPS * ROWS // SLOT_SENT)
    expert_ids = jax.vmap(lambda own, number: assign_block(jax.random.fold_in(keys[10], 2), own, number, SLOT_SENT, EXPERTS, TOP, CAP, 2))(expert_ids_keys, expert_ids_turns).reshape((STEPS, ROWS, TOP))
    gate_scores = jnp.clip(jnp.exp(math.log(1.0) - 2.3025851 * jax.random.uniform(keys[11], (STEPS, ROWS, TOP), jnp.float32) ** block_levels(keys[11], (STEPS, ROWS, TOP), ((1, 8),), -0.2, 0.2)), 0.1, 1.0)
    up_weight = gaussian(keys[12], (EXPERTS, D, FF), D ** -0.5, 0.125, ((0, 4), (2, 8)))
    down_weight = bell_draw_with(keys[13], (EXPERTS, FF, D), FF ** -0.5, 0.09375, ((0, 4), (1, 8)), (1, 2, 8, 2.0))
    return {"layer_input": layer_input, "queries": queries, "new_keys": new_keys, "new_values": new_values, "cache_keys": cache_keys, "cache_values": cache_values, "parents": parents, "lengths": lengths, "out_weight": out_weight, "norm_gain": norm_gain, "expert_ids": expert_ids, "gate_scores": gate_scores, "up_weight": up_weight, "down_weight": down_weight}


def attend_rows(query, past_keys, past_values, past_valid, own_key, own_value):
    total_rows = query.shape[0]
    key_all = jnp.concatenate([past_keys, own_key[:, None]], 1).astype(jnp.float32)
    value_all = jnp.concatenate([past_values, own_value[:, None]], 1).astype(jnp.float32)
    valid_all = jnp.concatenate([past_valid, jnp.ones((total_rows, 1), jnp.bool_)], 1)
    scores = jnp.einsum('rhe,rphe->rhp', query.astype(jnp.float32), key_all) * HEAD_DIM ** (-0.5)
    scores = jnp.where(valid_all[:, None, :], scores, -1e+30)
    shifted = jnp.exp(scores - lax.optimization_barrier(jnp.max(scores, axis=-1, keepdims=True)))
    weights = (shifted / lax.optimization_barrier(jnp.sum(shifted, axis=-1, keepdims=True))).astype(jnp.bfloat16)
    attended = jnp.einsum('rhp,rphe->rhe', weights.astype(jnp.float32), value_all)
    return attended.astype(jnp.bfloat16).reshape(total_rows, HEADS * HEAD_DIM)

def expert_mix(normed, chosen_ids, chosen_scores, up_weight, down_weight):
    total_rows = normed.shape[0]
    blocks = total_rows // SLOT_SENT
    choices_per = SLOT_SENT * TOP
    flat_ids = chosen_ids.reshape(blocks, choices_per)
    onehot = (flat_ids[:, :, None] == jnp.arange(EXPERTS, dtype=jnp.int32)[None, None, :]).astype(jnp.int32)
    before = lax.optimization_barrier(jnp.sum((jnp.cumsum(onehot, axis=1) - 1) * onehot, axis=2))
    position = flat_ids * CAP + before
    placed = (position[:, :, None] == jnp.arange(EXPERTS * CAP, dtype=jnp.int32)[None, None, :]).astype(jnp.float32)
    owners = (jnp.arange(choices_per, dtype=jnp.int32)[:, None] // TOP == jnp.arange(SLOT_SENT, dtype=jnp.int32)[None, :]).astype(jnp.float32)
    gate_share = (chosen_scores / lax.optimization_barrier(jnp.sum(chosen_scores, axis=-1, keepdims=True))).reshape(blocks, choices_per)
    dispatch = jnp.einsum('bas,ar->bsr', placed, owners, precision=lax.Precision.HIGHEST)
    combine = jnp.einsum('bas,ar->brs', placed * gate_share[:, :, None], owners, precision=lax.Precision.HIGHEST)
    buffered = jnp.einsum('bsr,brd->bsd', dispatch, normed.reshape(blocks, SLOT_SENT, D).astype(jnp.float32), precision=lax.Precision.HIGHEST).astype(jnp.bfloat16)
    by_expert = buffered.reshape(blocks, EXPERTS, CAP, D).transpose(1, 0, 2, 3).reshape(EXPERTS, blocks * CAP, D)

    def one_expert(operands):
        expert_rows, expert_up, expert_down = operands
        inner_units = jax.nn.relu(jnp.dot(expert_rows, expert_up, preferred_element_type=jnp.float32)).astype(jnp.bfloat16)
        inner_units = lax.optimization_barrier(inner_units)
        inner_units = inner_units.reshape(blocks * CAP, N_BEAM, FF // N_BEAM).astype(jnp.float32)
        pieces = jnp.einsum('rbf,bfd->rbd', inner_units, expert_down.reshape(N_BEAM, FF // N_BEAM, D).astype(jnp.float32))
        pieces = lax.optimization_barrier(pieces.astype(jnp.bfloat16))
        return lax.optimization_barrier(jnp.sum(pieces.astype(jnp.float32), axis=1))
    expert_out = lax.map(one_expert, (by_expert, up_weight, down_weight))
    expert_out = expert_out.reshape(EXPERTS, blocks, CAP, D).transpose(1, 0, 2, 3).reshape(blocks, EXPERTS * CAP, D)
    gated = jnp.einsum('brs,bsd->brd', combine, expert_out, precision=lax.Precision.HIGHEST)
    return gated.reshape(total_rows, D)

def reference(layer_input, queries, new_keys, new_values, cache_keys, cache_values, parents, lengths, out_weight, norm_gain, expert_ids, gate_scores, up_weight, down_weight):
    total_rows = BEAM * SENT
    sentence = jnp.arange(total_rows, dtype=jnp.int32) % SENT
    split_shape = (total_rows, HEADS, HEAD_DIM)
    past_keys = cache_keys.reshape(total_rows, PAST, HEADS, HEAD_DIM)
    past_values = cache_values.reshape(total_rows, PAST, HEADS, HEAD_DIM)
    row_lengths = jnp.take(lengths, sentence)
    past_valid = jnp.arange(PAST, dtype=jnp.int32)[None, :] < row_lengths[:, None]
    outputs = []
    for step_index in range(STEPS):
        source = (parents[step_index] * SENT + sentence).astype(jnp.int32)
        past_keys = jnp.take(past_keys, source, axis=0)
        past_values = jnp.take(past_values, source, axis=0)
        past_valid = jnp.take(past_valid, source, axis=0)
        own_key = new_keys[step_index].reshape(split_shape)
        own_value = new_values[step_index].reshape(split_shape)
        attended = attend_rows(queries[step_index].reshape(split_shape), past_keys, past_values, past_valid, own_key, own_value)
        hidden = layer_input[step_index].astype(jnp.float32) + jnp.dot(attended, out_weight, preferred_element_type=jnp.float32)
        center = hidden - lax.optimization_barrier(jnp.mean(hidden, axis=-1, keepdims=True))
        spread = lax.optimization_barrier(jnp.mean(center * center, axis=-1, keepdims=True))
        normed = (center * lax.rsqrt(spread + 1e-05) * norm_gain).astype(jnp.bfloat16)
        mixed = hidden + expert_mix(normed, expert_ids[step_index], gate_scores[step_index], up_weight, down_weight)
        outputs.append(mixed.astype(jnp.bfloat16))
        past_keys = jnp.concatenate([past_keys, own_key[:, None]], 1)
        past_values = jnp.concatenate([past_values, own_value[:, None]], 1)
        past_valid = jnp.concatenate([past_valid, jnp.ones((total_rows, 1), jnp.bool_)], 1)
    return jnp.stack(outputs)
```

```python
import functools

import jax
import jax.numpy as jnp
from jax import lax
from jax.experimental import pallas as pl
from jax.experimental.pallas import tpu as pltpu
from jax.sharding import PartitionSpec as P

HEAD_DIM = 128
TOP = 2
CAP = 2
BEAM = 4
STEPS = 2
MIB = 1 << 20
BF16 = jnp.bfloat16
F32 = jnp.float32
ANY = pl.ANY
VMEM = pltpu.VMEM


def call(kernel, name, limit, in_spaces, outs, args, scratch=(), bytes_moved=MIB, flops=0):
    return pl.pallas_call(
        kernel,
        name=name,
        out_shape=outs,
        in_specs=[pl.BlockSpec(memory_space=space) for space in in_spaces],
        out_specs=[pl.BlockSpec(memory_space=VMEM)] * len(outs),
        scratch_shapes=list(scratch),
        compiler_params=pltpu.CompilerParams(vmem_limit_bytes=limit),
        cost_estimate=pl.CostEstimate(flops=flops, bytes_accessed=bytes_moved, transcendentals=0),
    )(*args)


def shifted(value, axis, steps):
    count = lax.axis_size(axis)
    pairs = [(source, (source + steps) % count) for source in range(count)]
    return lax.ppermute(value, axis, pairs)


def other_core(value):
    count = lax.axis_size("beam")
    return lax.ppermute(value, "beam", [(source, source ^ 1) for source in range(count)])


def load_experts(weight, low, high, after):
    count = high - low
    rows = weight.shape[1] // 4

    def kernel(weight_ref, after_ref, out_ref, done_ref, sem):
        for index in range(count):
            for part in range(4):
                place = pl.ds(part * rows, rows)
                pltpu.make_async_copy(
                    weight_ref.at[low + index, place], out_ref.at[index, place], sem
                ).start()
        done_ref[...] = jnp.zeros_like(done_ref)
        pltpu.make_async_copy(weight_ref.at[pl.ds(low, count)], out_ref, sem).wait()

    shape = (count,) + weight.shape[1:]
    return call(
        kernel,
        "load_experts",
        MIB,
        [ANY, ANY],
        [pltpu.VMEM(shape, weight.dtype), jax.ShapeDtypeStruct((8, 128), F32)],
        [pltpu.with_memory_space_constraint(weight, pltpu.HBM), after],
        scratch=[pltpu.SemaphoreType.DMA],
        bytes_moved=2 * count * weight.shape[1] * weight.shape[2],
    )


def attend(keys, values, queries, own_keys, own_values, bias, waits):
    count = len(queries)
    rows, width = queries[0].shape
    heads = width // HEAD_DIM
    total = count * rows
    past = keys.shape[0]

    def kernel(*refs):
        key_ref, value_ref, bias_ref = refs[:3]
        parts = refs[3 : 3 + 3 * count]
        outs = refs[3 + 3 * count + len(waits) : 3 + 3 * count + len(waits) + count]
        q_ref, k_ref, v_ref = refs[-3:]
        for index in range(count):
            place = pl.ds(index * rows, rows)
            q_ref[place, :] = parts[index][...]
            k_ref[place, :] = parts[count + index][...]
            v_ref[place, :] = parts[2 * count + index][...]
        contract = (((1,), (1,)), ((), ()))
        for head in range(heads):
            cols = pl.ds(head * HEAD_DIM, HEAD_DIM)
            query = q_ref[:, cols]
            old = lax.dot_general(query, key_ref[:, cols], contract, preferred_element_type=F32)
            new = lax.dot_general(query, k_ref[:, cols], contract, preferred_element_type=F32)
            old = old * HEAD_DIM ** (-0.5) + bias_ref[:, pl.ds(0, past)]
            new = new * HEAD_DIM ** (-0.5) + bias_ref[:, pl.ds(past, total)]
            top = jnp.maximum(
                jnp.max(old, axis=-1, keepdims=True), jnp.max(new, axis=-1, keepdims=True)
            )
            old = jnp.exp(old - top)
            new = jnp.exp(new - top)
            norm = jnp.sum(old, axis=-1, keepdims=True) + jnp.sum(new, axis=-1, keepdims=True)
            old = (old / norm).astype(BF16)
            new = (new / norm).astype(BF16)
            out = jnp.dot(old, value_ref[:, cols], preferred_element_type=F32) + jnp.dot(
                new, v_ref[:, cols], preferred_element_type=F32
            )
            out = out.astype(BF16)
            for index in range(count):
                outs[index][:, cols] = out[index * rows : (index + 1) * rows, :]

    return call(
        kernel,
        "attend",
        8 * MIB,
        [VMEM] * (3 + 3 * count) + [ANY] * len(waits),
        [jax.ShapeDtypeStruct((rows, width), BF16)] * count,
        [keys, values, bias, *queries, *own_keys, *own_values, *waits],
        scratch=[pltpu.VMEM((total, width), BF16)] * 3,
    )


def project(select, chunks, weight, pieces, waits):
    count = len(chunks)
    rows, width = chunks[0].shape
    model = weight.shape[1]
    size = rows // pieces

    def kernel(*refs):
        select_ref, weight_ref = refs[:2]
        parts = refs[2 : 2 + count]
        own_ref = refs[2 + count + len(waits)]
        sent = refs[3 + count + len(waits) : 2 + count + len(waits) + pieces]
        all_ref = refs[-1]
        for index in range(count):
            all_ref[pl.ds(index * rows, rows), :] = parts[index][...]
        picked = jnp.dot(select_ref[...], all_ref[...], preferred_element_type=F32).astype(BF16)
        product = jnp.dot(picked, weight_ref[...], preferred_element_type=F32)
        own_ref[...] = product[:size, :]
        for piece in range(1, pieces):
            sent[piece - 1][...] = product[piece * size : (piece + 1) * size, :].astype(BF16)

    return call(
        kernel,
        "project",
        6 * MIB,
        [VMEM] * (2 + count) + [ANY] * len(waits),
        [jax.ShapeDtypeStruct((size, model), F32)]
        + [jax.ShapeDtypeStruct((size, model), BF16)] * (pieces - 1),
        [select, weight, *chunks, *waits],
        scratch=[pltpu.VMEM((count * rows, width), BF16)],
    )


def normalize(entry, own, others, gain, waits):
    size, model = own.shape

    def kernel(*refs):
        entry_ref, gain_ref, own_ref = refs[:3]
        parts = refs[3 : 3 + len(others)]
        hidden_ref, normed_ref = refs[-2:]
        hidden = own_ref[...]
        for part in parts:
            hidden = hidden + part[...].astype(F32)
        hidden = entry_ref[...] + hidden
        center = hidden - jnp.mean(hidden, axis=-1, keepdims=True)
        spread = jnp.mean(center * center, axis=-1, keepdims=True)
        hidden_ref[...] = hidden
        normed_ref[...] = (center * lax.rsqrt(spread + 1e-05) * gain_ref[...]).astype(BF16)

    return call(
        kernel,
        "normalize",
        4 * MIB,
        [VMEM] * (3 + len(others)) + [ANY] * len(waits),
        [jax.ShapeDtypeStruct((size, model), F32), jax.ShapeDtypeStruct((size, model), BF16)],
        [entry, gain, own, *others, *waits],
    )


def expert_up(dispatch, blocks, weights, waits):
    slots, total = dispatch.shape
    rows, model = blocks[0].shape
    count = len(blocks)
    local = sum(weight.shape[0] for weight in weights)
    per = slots // local
    width = weights[0].shape[2]

    def kernel(*refs):
        dispatch_ref = refs[0]
        parts = refs[1 : 1 + count]
        held = refs[1 + count : 1 + count + len(weights)]
        out_ref, all_ref, sorted_ref = refs[-3:]
        for index in range(count):
            all_ref[pl.ds(index * rows, rows), :] = parts[index][...]
        sorted_ref[...] = jnp.dot(
            dispatch_ref[...], all_ref[...], preferred_element_type=F32
        ).astype(BF16)
        expert = 0
        for weight_ref in held:
            for index in range(weight_ref.shape[0]):
                place = pl.ds(expert * per, per)
                inner = jnp.dot(
                    sorted_ref[place, :], weight_ref[index], preferred_element_type=F32
                )
                out_ref[place, :] = jnp.maximum(inner, 0.0).astype(BF16)
                expert += 1

    return call(
        kernel,
        "expert_up",
        6 * MIB,
        [VMEM] * (1 + count + len(weights)) + [ANY] * len(waits),
        [jax.ShapeDtypeStruct((slots, width), BF16)],
        [
            dispatch,
            *blocks,
            *[pltpu.with_memory_space_constraint(weight, pltpu.VMEM) for weight in weights],
            *waits,
        ],
        scratch=[pltpu.VMEM((total, model), BF16), pltpu.VMEM((slots, model), BF16)],
        flops=2 * slots * model * width,
    )[0]


def expert_down(combine, inner, weights, whole, low):
    rows, slots = combine.shape[1:]
    local = whole.shape[0]
    per = slots // local
    model = whole.shape[2]
    half = rows // 2
    late = local - low

    def kernel(*refs):
        combine_ref, inner_ref, whole_ref = refs[:3]
        held = refs[3 : 3 + len(weights)]
        mine_ref, theirs_ref, late_ref, out_ref, sem = refs[-5:]
        arriving = [
            pltpu.make_async_copy(whole_ref.at[low + index], late_ref.at[index], sem.at[index])
            for index in range(late)
        ]
        for copy in arriving:
            copy.start()
        pairs = [(ref, index) for ref in held for index in range(ref.shape[0])]
        pairs += [(late_ref, index) for index in range(late)]
        for expert, (ref, index) in enumerate(pairs):
            if expert >= low:
                arriving[expert - low].wait()
            place = pl.ds(expert * per, per)
            out_ref[place, :] = jnp.dot(
                inner_ref[place, :], ref[index], preferred_element_type=F32
            ).astype(BF16)
        for target, start in ((theirs_ref, half), (mine_ref, 0)):
            place = pl.ds(start, half)
            total = jnp.dot(combine_ref[0, place, :], out_ref[...], preferred_element_type=F32)
            total += jnp.dot(combine_ref[1, place, :], out_ref[...], preferred_element_type=F32)
            target[...] = total.astype(BF16)

    return call(
        kernel,
        "expert_down",
        16 * MIB,
        [VMEM, VMEM, ANY] + [VMEM] * len(weights),
        [jax.ShapeDtypeStruct((half, model), BF16)] * 2,
        [
            combine,
            inner,
            pltpu.with_memory_space_constraint(whole, pltpu.HBM),
            *[pltpu.with_memory_space_constraint(weight, pltpu.VMEM) for weight in weights],
        ],
        scratch=[
            pltpu.VMEM((max(1, late),) + whole.shape[1:], BF16),
            pltpu.VMEM((slots, model), BF16),
            pltpu.SemaphoreType.DMA((max(1, late),)),
        ],
        flops=2 * slots * model * whole.shape[1],
    )


def add_pair(mine, theirs, count):
    total, model = mine.shape
    rows = total // count

    def kernel(mine_ref, theirs_ref, *outs):
        for index in range(count):
            place = pl.ds(index * rows, rows)
            outs[index][...] = (
                mine_ref[place, :].astype(F32) + theirs_ref[place, :].astype(F32)
            ).astype(BF16)

    return call(
        kernel,
        "add_pair",
        6 * MIB,
        [VMEM, VMEM],
        [jax.ShapeDtypeStruct((rows, model), BF16)] * count,
        [mine, theirs],
    )


def gather_sums(place_z, blocks, hidden, pieces):
    rows, model = blocks[0].shape
    size = rows // pieces
    width = model // pieces
    count = len(blocks)

    def kernel(*refs):
        z_ref = refs[0]
        parts = refs[1 : 1 + count]
        hidden_ref = refs[1 + count]
        own_ref = refs[2 + count]
        sent = refs[3 + count : 2 + count + pieces]
        total_ref = refs[-1]
        mine = z_ref[0]
        total = parts[0][...].astype(F32)
        for part in parts[1:]:
            total = total + part[...].astype(F32)
        spread = jnp.concatenate([hidden_ref[...]] * pieces, 0)
        owner = lax.broadcasted_iota(jnp.int32, (rows, model), 0) // size
        total_ref[...] = total + jnp.where(owner == mine, spread, 0.0)
        for piece in range(pieces):
            start = pl.multiple_of(lax.rem(mine + piece, pieces) * width, 128)
            cut = total_ref[:, pl.ds(start, width)]
            if piece == 0:
                own_ref[...] = cut
            else:
                sent[piece - 1][...] = cut.astype(BF16)

    return call(
        kernel,
        "gather_sums",
        4 * MIB,
        [pltpu.SMEM] + [VMEM] * (count + 1),
        [jax.ShapeDtypeStruct((rows, width), F32)]
        + [jax.ShapeDtypeStruct((rows, width), BF16)] * (pieces - 1),
        [place_z, *blocks, hidden],
        scratch=[pltpu.VMEM((rows, model), F32)],
    )


def attention_bias(parents, lengths, my_slot, first_sent, sents, past):
    slots = (my_slot - jnp.arange(BEAM, dtype=jnp.int32)) % BEAM
    sent_total = lengths.shape[0]
    my_lengths = lax.dynamic_slice_in_dim(lengths, first_sent, sents, 0)
    table = lax.dynamic_slice_in_dim(
        parents.reshape(STEPS, BEAM, sent_total), first_sent, sents, 2
    )
    later = sum(
        jnp.where((slots == slot)[:, None], table[1, slot][None, :], 0) for slot in range(BEAM)
    )
    rank = jnp.arange(sents, dtype=jnp.int32)
    same = rank[:, None] == rank[None, :]
    seen = jnp.arange(past, dtype=jnp.int32)[None, :] < my_lengths[:, None]
    old = same[:, :, None] & seen[None, :, :]
    old = jnp.broadcast_to(
        old.reshape(1, sents, sents * past), (BEAM * STEPS, sents, sents * past)
    ).reshape(BEAM * STEPS * sents, sents * past)
    step = jnp.arange(STEPS, dtype=jnp.int32)
    shape = (BEAM, STEPS, sents, BEAM, STEPS, sents)
    own = (slots[:, None] == slots[None, :])[:, None, None, :, None, None] & (
        step[:, None] == step[None, :]
    )[None, :, None, None, :, None]
    before = (
        (step == 1)[None, :, None, None, None, None]
        & (step == 0)[None, None, None, None, :, None]
        & (later[:, :, None] == slots[None, None, :])[:, None, :, :, None, None]
    )
    new = (own | before) & same[None, None, :, None, None, :]
    new = jnp.broadcast_to(new, shape).reshape(old.shape[0], BEAM * STEPS * sents)
    allowed = jnp.concatenate([old, new], 1)
    first = sum(
        jnp.where((my_slot == slot), table[0, slot], 0) for slot in range(BEAM)
    )
    mine = sum(jnp.where((my_slot == slot), table[1, slot], 0) for slot in range(BEAM))
    second = sum(jnp.where(mine == slot, table[0, slot], 0) for slot in range(BEAM))
    holder = (jnp.concatenate([first, second]) - my_slot) % BEAM
    return jnp.where(allowed, 0.0, -1e30).astype(F32), holder


def body(
    layer_input,
    queries,
    new_keys,
    new_values,
    cache_keys,
    cache_values,
    parents,
    lengths,
    out_weight,
    norm_gain,
    expert_ids,
    gate_scores,
    up_weight,
    down_weight,
):
    beams = lax.axis_size("beam")
    zs = lax.axis_size("expert")
    chips = beams // 2
    spacing = beams // BEAM
    beam_index = lax.axis_index("beam")
    my_z = lax.axis_index("expert")
    my_slot = beam_index // spacing
    sents, past, width = cache_keys.shape
    rows = STEPS * sents
    size = rows // zs
    model = layer_input.shape[2]
    local = up_weight.shape[0]
    first_sent = beam_index % spacing * sents

    fresh = [part.reshape(rows, width) for part in (queries, new_keys, new_values)]
    spread = [[part] for part in fresh]
    for shift in range(1, BEAM):
        for place, part in enumerate(fresh):
            spread[place].append(shifted(part, "beam", shift * spacing))
    half = max(1, local // 2)
    deep = max(half, local - local // 4)
    up_low, up_low_done = load_experts(up_weight, 0, half, queries)

    bias, holder = attention_bias(parents, lengths, my_slot, first_sent, sents, past)
    rank = jnp.arange(rows, dtype=jnp.int32)
    wanted = (rank + my_z * size) % rows
    source = (
        jnp.sum(jnp.where(wanted[:, None] == rank[None, :], holder[None, :], 0), 1) * rows + wanted
    )
    select = (source[:, None] == jnp.arange(BEAM * rows, dtype=jnp.int32)[None, :]).astype(BF16)

    share = gate_scores / jnp.sum(gate_scores, axis=-1, keepdims=True)
    routing = jnp.concatenate([expert_ids.astype(F32), share], -1).reshape(rows, 2 * TOP)
    routes = [routing] + [shifted(routing, "beam", 2 * shift) for shift in range(1, chips)]
    routes = jnp.stack(routes)
    routes = jnp.concatenate([routes, other_core(routes)], 0)

    chunks = attend(
        cache_keys.reshape(sents * past, width),
        cache_values.reshape(sents * past, width),
        *spread,
        bias,
        [up_low_done],
    )
    returned = [chunks[0]] + [
        shifted(chunks[shift], "beam", -shift * spacing) for shift in range(1, BEAM)
    ]
    up_high, up_high_done = load_experts(up_weight, half, local, chunks[0])
    sums = project(select, returned, out_weight, zs, [up_high_done])
    others = [shifted(sums[shift], "expert", shift) for shift in range(1, zs)]
    down_low, down_low_done = load_experts(down_weight, 0, half, sums[0])
    entry = lax.dynamic_slice_in_dim(
        layer_input.reshape(rows, model), my_z * size, size, 0
    ).astype(F32)
    hidden, normed = normalize(entry, sums[0], others, norm_gain[None, :], [down_low_done])

    column = [normed] + [shifted(normed, "expert", shift) for shift in range(1, zs)]
    downs = [down_low]
    waits = []
    if deep > half:
        down_high, down_high_done = load_experts(down_weight, half, deep, normed)
        downs.append(down_high)
        waits.append(down_high_done)
    column = jnp.concatenate(column, 0)
    blocks = [column] + [shifted(column, "beam", 2 * shift) for shift in range(1, chips)]
    blocks = blocks + [other_core(block) for block in blocks]

    ids = routes[:, :, :TOP].astype(jnp.int32)
    shares = routes[:, :, TOP:]
    flat = ids.reshape(beams, STEPS, sents * TOP)
    order = jnp.arange(sents * TOP, dtype=jnp.int32)
    repeats = (flat[:, :, :, None] == flat[:, :, None, :]) & (order[:, None] > order[None, :])
    before = jnp.sum(repeats.astype(jnp.int32), -1)
    group = jnp.arange(beams * STEPS, dtype=jnp.int32).reshape(beams, STEPS, 1)
    per = beams * STEPS * CAP
    slot = (flat - my_z * local) * per + group * CAP + before
    slot = slot.reshape(beams * rows, TOP)
    slots = jnp.arange(local * per, dtype=jnp.int32)
    natural = slots[None, :, None] == slot[:, None, :]
    gates = jnp.sum(jnp.where(natural, shares.reshape(beams * rows, 1, TOP), 0.0), -1)
    gates_high = gates.astype(BF16)
    gates_low = (gates - gates_high.astype(F32)).astype(BF16)
    combine = jnp.stack([gates_high, gates_low])
    turned = slot.reshape(beams, zs, size, TOP)
    turned = jnp.stack(
        [
            lax.dynamic_index_in_dim(turned, (my_z - shift) % zs, 1, keepdims=False)
            for shift in range(zs)
        ],
        1,
    ).reshape(beams * rows, TOP)
    dispatch = (
        (slots[:, None] == turned[None, :, 0]) | (slots[:, None] == turned[None, :, 1])
    ).astype(BF16)

    inner = expert_up(dispatch, blocks, [up_low, up_high], waits)
    mine, theirs = expert_down(combine, inner, downs, down_weight, deep)

    sums = add_pair(mine, other_core(theirs), chips)
    sums = [sums[0]] + [shifted(sums[shift], "beam", -2 * shift) for shift in range(1, chips)]
    cuts = gather_sums(my_z.astype(jnp.int32)[None], sums, hidden, zs)
    mixed = cuts[0]
    for shift in range(1, zs):
        mixed = mixed + shifted(cuts[shift], "expert", shift).astype(F32)
    return mixed.astype(BF16).reshape(STEPS, sents, width)


def solution(mesh):
    return jax.shard_map(
        body,
        mesh=mesh,
        in_specs=(
            P(None, "beam", None),
            P(None, "beam", "expert"),
            P(None, "beam", "expert"),
            P(None, "beam", "expert"),
            P("beam", None, "expert"),
            P("beam", None, "expert"),
            P(),
            P(),
            P("expert", None),
            P(),
            P(None, "beam", None),
            P(None, "beam", None),
            P("expert", None, "beam"),
            P("expert", "beam", None),
        ),
        out_specs=P(None, "beam", "expert"),
        check_vma=False,
    )
```

```python
import math

import jax
import jax.numpy as jnp
from jax import lax
from jax.experimental import pallas as pl
from jax.experimental.pallas import tpu as pltpu
from jax.sharding import PartitionSpec as P

HEAD_DIM = 128
TOP = 2
CAP = 2
BEAM = 4
STEPS = 2
HELD = 5
MIDDLE = 1
STAGES = (0, 2, 5, 9, 13)
MIB = 1 << 20
BF16 = jnp.bfloat16
F32 = jnp.float32
ANY = pl.ANY
VMEM = pltpu.VMEM


def call(
    kernel, name, limit, in_spaces, outs, args, scratch=(), bytes_moved=MIB, flops=0, aliases=None
):
    return pl.pallas_call(
        kernel,
        name=name,
        out_shape=outs,
        in_specs=[pl.BlockSpec(memory_space=space) for space in in_spaces],
        out_specs=[pl.BlockSpec(memory_space=VMEM)] * len(outs),
        scratch_shapes=list(scratch),
        input_output_aliases=aliases or {},
        compiler_params=pltpu.CompilerParams(vmem_limit_bytes=limit),
        cost_estimate=pl.CostEstimate(flops=flops, bytes_accessed=bytes_moved, transcendentals=0),
    )(*args)


def swapped(value, axis, mask):
    count = lax.axis_size(axis)
    return lax.ppermute(value, axis, [(source, source ^ mask) for source in range(count)])


def exchanged(pieces, axis, unit):
    got = [swapped(pieces[index], axis, index * unit) for index in reversed(range(1, len(pieces)))]
    return [pieces[0]] + got[::-1]


def split_index(index, size):
    assert size & (size - 1) == 0
    return index >> (size.bit_length() - 1), index & (size - 1)


def here(sents):
    beam = lax.axis_index("beam")
    slot, rest = split_index(beam, lax.axis_size("beam") // BEAM)
    return slot, rest * sents


def iota(shape, dim):
    return lax.broadcasted_iota(jnp.int32, shape, dim)


def one_hot(condition):
    return jnp.where(condition, 1.0, 0.0).astype(BF16)


def pack(queries, new_keys, new_values, small):
    steps, sents, width = queries.shape
    parts = (queries, new_keys, new_values)
    count = len(parts)

    def kernel(*refs):
        sources = refs[: count + len(small)]
        out_ref = refs[count + len(small)]
        targets = refs[count + len(small) + 1 : -1]
        sem = refs[-1]
        copies = [
            (sources[place].at[step], out_ref.at[pl.ds((place * steps + step) * sents, sents)])
            for place in range(count)
            for step in range(steps)
        ]
        copies += list(zip(sources[count:], targets))
        copies = [
            pltpu.make_async_copy(source, target, sem.at[index])
            for index, (source, target) in enumerate(copies)
        ]
        for copy in copies:
            copy.start()
        for copy in copies:
            copy.wait()

    return call(
        kernel,
        "pack",
        MIB // 2,
        [ANY] * (count + len(small)),
        [pltpu.VMEM((count * steps * sents, width), BF16)]
        + [pltpu.VMEM(array.shape, array.dtype) for array in small],
        [pltpu.with_memory_space_constraint(part, pltpu.HBM) for part in (*parts, *small)],
        scratch=[pltpu.SemaphoreType.DMA((count * steps + len(small),))],
    )


def masks(parents, lengths, expert_ids, gate_scores, past):
    steps, _, sents = expert_ids.shape
    rows = steps * sents
    sent_total = lengths.shape[1]
    asked = BEAM * rows
    span = sents * past

    def kernel(*refs):
        parent_ref, length_ref, id_ref, gate_ref = refs[:4]
        bias_ref, select_ref, route_ref, place_ref = refs[4:]
        place_ref[...] = jnp.full((8, 128), lax.axis_index("expert"), jnp.int32)
        my_slot, first = here(sents)
        turn, rest = split_index(iota((asked, 1), 0), rows)
        step, rank = split_index(rest, sents)
        slot = my_slot ^ turn
        table = parent_ref[...].astype(F32).astype(BF16)
        contract = (((1,), (1,)), ((), ()))
        everyone = iota((asked, BEAM * sent_total), 1)
        source = one_hot(everyone == slot * sent_total + first + rank)
        found = lax.dot_general(source, table, contract, preferred_element_type=F32)
        before = found[:, 1:2].astype(jnp.int32)
        counts = length_ref[...].astype(F32).astype(BF16)
        sentence = one_hot(iota((asked, sent_total), 1) == first + rank)
        counts = jnp.broadcast_to(counts, (8, sent_total))
        valid = lax.dot_general(sentence, counts, contract, preferred_element_type=F32)
        valid = valid[:, 0:1].astype(jnp.int32)
        cached_sent, position = split_index(iota((asked, span), 1), past)
        bias_ref[:, pl.ds(0, span)] = jnp.where(
            (cached_sent == rank) & (position < valid), 0.0, -1e30
        )
        key_turn, key_rest = split_index(iota((asked, asked), 1), rows)
        key_step, key_rank = split_index(key_rest, sents)
        key_slot = my_slot ^ key_turn
        own = (key_turn == turn) & (key_step == step)
        earlier = (step == 1) & (key_step == 0) & (key_slot == before)
        bias_ref[:, pl.ds(span, asked)] = jnp.where(
            (key_rank == rank) & (own | earlier), 0.0, -1e30
        )
        chain = one_hot(
            everyone[:rows] == jnp.where(step[:rows] == 0, my_slot, before[:rows]) * sent_total
            + first
            + rank[:rows]
        )
        holder = lax.dot_general(chain, table, contract, preferred_element_type=F32)
        holder = holder[:, 0:1].astype(jnp.int32)
        holder = holder ^ my_slot
        select_ref[...] = one_hot(
            iota((rows, asked), 1) == holder * rows + iota((rows, asked), 0)
        )
        lane = iota((sents, 128), 1)
        square = iota((sents, sents), 0) == iota((sents, sents), 1)
        for step in range(steps):
            columns = []
            for part in (id_ref[step].astype(F32), gate_ref[step]):
                for choice in range(TOP):
                    line = jnp.where(square, part[choice : choice + 1, :], 0.0)
                    columns.append(jnp.sum(line, axis=1, keepdims=True))
            scores = columns[TOP:]
            share = [score / sum(scores) for score in scores]
            high = [part.astype(BF16).astype(F32) for part in share]
            columns[TOP:] = high + [part - top for part, top in zip(share, high)]
            route = jnp.zeros((sents, 128), F32)
            for index, column in enumerate(columns):
                route = jnp.where(lane == index, column, route)
            route_ref[pl.ds(step * sents, sents), :] = route.astype(BF16)

    return call(
        kernel,
        "masks",
        2 * MIB,
        [VMEM] * 4,
        [
            pltpu.VMEM((asked, span + asked), F32),
            pltpu.VMEM((rows, asked), BF16),
            pltpu.VMEM((rows, 128), BF16),
            pltpu.VMEM((8, 128), jnp.int32),
        ],
        [parents, lengths, expert_ids, gate_scores],
    )


def routing(place, mine, theirs, local, steps, sents, waits):
    total = 2 * mine.shape[0]
    rows = steps * sents
    beams = total // rows
    per = beams * steps * CAP
    slots = local * per
    step_rows = 128

    def kernel(*refs):
        place_ref, mine_ref, theirs_ref = refs[:3]
        dispatch_ref, combine_ref, gate_ref = refs[-3:]
        by_slot = jnp.zeros((slots, 1), F32)
        my_z = place_ref[0:1, 0:1]
        for start in range(0, total, step_rows):
            half, ref = divmod(start, total // 2)
            info = (theirs_ref if half else mine_ref)[pl.ds(ref, step_rows), :].astype(F32)
            turned = jnp.transpose(info)
            row = iota((step_rows, step_rows), 0)
            lane = iota((step_rows, step_rows), 1)
            earlier = (split_index(row, sents)[0] == split_index(lane, sents)[0]) & (lane < row)
            group = split_index(iota((step_rows, 1), 0) + start, sents)[0]
            columns = iota((step_rows, slots), 1)
            hits = []
            for choice in range(TOP):
                ids = info[:, choice : choice + 1]
                same = jnp.zeros((step_rows, step_rows), F32)
                for other in range(TOP):
                    same += jnp.where(earlier & (turned[other : other + 1, :] == ids), 1.0, 0.0)
                before = jnp.sum(same, axis=1, keepdims=True).astype(jnp.int32)
                slot = (ids.astype(jnp.int32) - my_z * local) * per + group * CAP + before
                hits.append(columns == slot)
            gates = jnp.zeros((step_rows, slots), F32)
            for choice in range(TOP):
                high, low = TOP + choice, 2 * TOP + choice
                share = info[:, high : high + 1] + info[:, low : low + 1]
                gates = jnp.where(hits[choice], share, gates)
            by_slot += jnp.sum(jnp.transpose(gates), axis=1, keepdims=True)
            natural = one_hot(hits[0] | hits[1])
            combine_ref[pl.ds(start, step_rows), :] = natural
            dispatch_ref[:, pl.ds(start, step_rows)] = jnp.transpose(
                natural.astype(F32)
            ).astype(BF16)
        gate_ref[...] = jnp.broadcast_to(by_slot, (slots, 128))

    return call(
        kernel,
        "routing",
        max(2, total // 128) * MIB,
        [VMEM, VMEM, VMEM] + [ANY] * len(waits),
        [
            jax.ShapeDtypeStruct((slots, total), BF16),
            jax.ShapeDtypeStruct((total, slots), BF16),
            jax.ShapeDtypeStruct((slots, 128), F32),
        ],
        [place, mine, theirs, *waits],
    )


def stack_rows(parts, waits):
    rows, width = parts[0].shape

    def kernel(*refs):
        for index in range(len(parts)):
            refs[-1][pl.ds(index * rows, rows), :] = refs[index][...]

    return call(
        kernel,
        "stack_rows",
        MIB,
        [VMEM] * len(parts) + [ANY] * len(waits),
        [jax.ShapeDtypeStruct((len(parts) * rows, width), parts[0].dtype)],
        [*parts, *waits],
    )[0]


def bring(pieces, after):
    count = len(pieces)
    shapes = [array.shape if index is None else array.shape[1:] for array, index in pieces]

    def kernel(*refs):
        targets = refs[count + 1 : 2 * count + 1]
        done_ref, sem = refs[-2:]
        moves = []
        for place, (_, index) in enumerate(pieces):
            source = refs[place] if index is None else refs[place].at[index]
            moves.append(pltpu.make_async_copy(source, targets[place], sem.at[place]))
        for move in moves:
            move.start()
        done_ref[...] = jnp.zeros_like(done_ref)
        for move in moves:
            move.wait()

    *brought, done = call(
        kernel,
        "bring",
        MIB // 2,
        [ANY] * (count + 1),
        [pltpu.VMEM(shape, array.dtype) for shape, (array, _) in zip(shapes, pieces)]
        + [jax.ShapeDtypeStruct((8, 128), F32)],
        [pltpu.with_memory_space_constraint(array, pltpu.HBM) for array, _ in pieces] + [after],
        scratch=[pltpu.SemaphoreType.DMA((max(1, count),))],
        bytes_moved=4 * sum(math.prod(shape) for shape in shapes),
    )
    return brought, done


def attend(keys, values, messages, bias, route, waits):
    count = len(messages)
    rows = route.shape[0]
    steps, sents = STEPS, rows // STEPS
    width = messages[0].shape[1]
    heads = width // HEAD_DIM
    total = count * rows
    past = keys.shape[1]
    routed = sents if width >= steps * 128 else 0

    def kernel(*refs):
        key_ref, value_ref, bias_ref, route_ref = refs[:4]
        parts = refs[4 : 4 + count]
        outs = refs[4 + count + len(waits) : 4 + 2 * count + len(waits)]
        q_ref, k_ref, v_ref = refs[-3:]
        for index, part in enumerate(parts):
            place = pl.ds(index * rows, rows)
            q_ref[place, :] = part[pl.ds(0, rows), :]
            k_ref[place, :] = part[pl.ds(rows, rows), :]
            v_ref[place, :] = part[pl.ds(2 * rows, rows), :]
        if routed:
            for out in outs:
                out[pl.ds(rows, sents), :] = jnp.zeros((sents, width), BF16)
                for step in range(steps):
                    out[pl.ds(rows, sents), pl.ds(step * 128, 128)] = route_ref[
                        pl.ds(step * sents, sents), :
                    ]
        contract = (((1,), (1,)), ((), ()))
        for head in range(heads):
            cols = pl.ds(head * HEAD_DIM, HEAD_DIM)
            query = q_ref[:, cols]
            old = lax.dot_general(query, key_ref[0, :, cols], contract, preferred_element_type=F32)
            new = lax.dot_general(query, k_ref[:, cols], contract, preferred_element_type=F32)
            old = old * HEAD_DIM ** (-0.5) + bias_ref[:, pl.ds(0, past)]
            new = new * HEAD_DIM ** (-0.5) + bias_ref[:, pl.ds(past, total)]
            top = jnp.maximum(
                jnp.max(old, axis=-1, keepdims=True), jnp.max(new, axis=-1, keepdims=True)
            )
            old = jnp.exp(old - top)
            new = jnp.exp(new - top)
            norm = jnp.sum(old, axis=-1, keepdims=True) + jnp.sum(new, axis=-1, keepdims=True)
            old = (old / norm).astype(BF16)
            new = (new / norm).astype(BF16)
            out = jnp.dot(old, value_ref[0, :, cols], preferred_element_type=F32) + jnp.dot(
                new, v_ref[:, cols], preferred_element_type=F32
            )
            out = out.astype(BF16)
            for index in range(count):
                outs[index][pl.ds(0, rows), cols] = out[index * rows : (index + 1) * rows, :]

    return call(
        kernel,
        "attend",
        2 * MIB,
        [VMEM] * (4 + count) + [ANY] * len(waits),
        [jax.ShapeDtypeStruct((rows + routed, width), BF16)] * count,
        [keys, values, bias, route, *messages, *waits],
        scratch=[pltpu.VMEM((total, width), BF16)] * 3,
    )


def project(select, chunks, weight, sents, waits):
    count = len(chunks)
    width = chunks[0].shape[1]
    rows = select.shape[0]
    steps = rows // sents
    model = weight.shape[2]
    routed = chunks[0].shape[0] > rows

    def kernel(*refs):
        select_ref, weight_ref = refs[:2]
        parts = refs[2 : 2 + count]
        own_ref, sent_ref, route_ref, all_ref = refs[-4:]
        for index in range(count):
            all_ref[pl.ds(index * rows, rows), :] = parts[index][pl.ds(0, rows), :]
        picked = jnp.dot(select_ref[...], all_ref[...], preferred_element_type=F32).astype(BF16)
        product = jnp.dot(picked, weight_ref[0], preferred_element_type=F32)
        own_ref[...] = product
        sent_ref[...] = product.astype(BF16)
        for index in range(count):
            for step in range(steps):
                place = pl.ds(index * rows + step * sents, sents)
                if routed:
                    route_ref[place, :] = parts[index][pl.ds(rows, sents), pl.ds(step * 128, 128)]
                else:
                    route_ref[place, :] = jnp.zeros((sents, 128), BF16)

    return call(
        kernel,
        "project",
        2 * MIB,
        [VMEM] * (2 + count) + [ANY] * len(waits),
        [
            jax.ShapeDtypeStruct((rows, model), F32),
            jax.ShapeDtypeStruct((rows, model), BF16),
            jax.ShapeDtypeStruct((count * rows, 128), BF16),
        ],
        [select, weight, *chunks, *waits],
        scratch=[pltpu.VMEM((count * rows, width), BF16)],
    )


def normalize(entry, own, others, gain, waits):
    rows, model = own.shape
    steps, sents, _ = entry.shape

    def kernel(*refs):
        entry_ref, gain_ref, own_ref = refs[:3]
        parts = refs[3 : 3 + len(others)]
        hidden_ref, normed_ref = refs[-2:]
        for step in range(steps):
            place = pl.ds(step * sents, sents)
            hidden = own_ref[place, :]
            for part in parts:
                hidden = hidden + part[place, :].astype(F32)
            hidden = entry_ref[step].astype(F32) + hidden
            center = hidden - jnp.mean(hidden, axis=-1, keepdims=True)
            spread = jnp.mean(center * center, axis=-1, keepdims=True)
            hidden_ref[place, :] = hidden
            normed_ref[place, :] = (center * lax.rsqrt(spread + 1e-05) * gain_ref[...]).astype(
                BF16
            )

    return call(
        kernel,
        "normalize",
        MIB,
        [VMEM] * (3 + len(others)) + [ANY] * len(waits),
        [jax.ShapeDtypeStruct((rows, model), F32), jax.ShapeDtypeStruct((rows, model), BF16)],
        [entry, gain, own, *others, *waits],
    )


def expert_up(dispatch, blocks, weights, first, local, array, later, after):
    per = dispatch.shape[0] // local
    total = dispatch.shape[1]
    rows, model = blocks[0].shape
    count = len(blocks)
    width = weights[0].shape[1]
    slots = per * len(weights)
    late = len(later)

    def kernel(*refs):
        dispatch_ref, later_ref = refs[:2]
        parts = refs[2 : 2 + count]
        weight_refs = refs[2 + count : 2 + count + len(weights)]
        targets = refs[3 + count + len(weights) : 3 + count + len(weights) + late]
        out_ref, all_ref, sorted_ref, sem = refs[-4:]
        moves = [
            pltpu.make_async_copy(later_ref.at[index], targets[place], sem.at[place])
            for place, index in enumerate(later)
        ]
        for move in moves:
            move.start()
        for index in range(count):
            all_ref[pl.ds(index * rows, rows), :] = parts[index][...]
        sorted_ref[...] = jnp.dot(
            dispatch_ref[pl.ds(first * per, slots), :],
            all_ref[...],
            preferred_element_type=F32,
        ).astype(BF16)
        for expert, weight_ref in enumerate(weight_refs):
            place = pl.ds(expert * per, per)
            inner = jnp.dot(sorted_ref[place, :], weight_ref[...], preferred_element_type=F32)
            out_ref[place, :] = jnp.maximum(inner, 0.0).astype(BF16)
        for move in moves:
            move.wait()

    *brought, inner = call(
        kernel,
        "expert_up",
        2 * (total + slots) * model + MIB,
        [VMEM, ANY] + [VMEM] * (count + len(weights)) + [ANY],
        [pltpu.VMEM(array.shape[1:], BF16)] * late + [pltpu.VMEM((slots, width), BF16)],
        [
            dispatch,
            pltpu.with_memory_space_constraint(array, pltpu.HBM),
            *blocks,
            *[pltpu.with_memory_space_constraint(weight, pltpu.VMEM) for weight in weights],
            after,
        ],
        scratch=[
            pltpu.VMEM((total, model), BF16),
            pltpu.VMEM((slots, model), BF16),
            pltpu.SemaphoreType.DMA((max(1, late),)),
        ],
        bytes_moved=2 * len(weights) * model * width,
        flops=2 * slots * model * width,
    )
    return brought, inner


def expert_down(combine, gates, inners, weights, array, late):
    rows, slots = combine.shape
    depth, model = array.shape[1:]
    per = slots // (len(weights) + len(late))
    half = rows // 2
    counts = [inner.shape[0] // per for inner in inners]

    def kernel(*refs):
        combine_ref, gate_ref, array_ref = refs[:3]
        inner_refs = refs[3 : 3 + len(inners)]
        weight_refs = refs[3 + len(inners) : 3 + len(inners) + len(weights)]
        mine_ref, theirs_ref, late_ref, out_ref, sem = refs[-5:]
        moves = [
            pltpu.make_async_copy(array_ref.at[index], late_ref.at[place], sem.at[place])
            for place, index in enumerate(late)
        ]
        for move in moves:
            move.start()
        sources = [
            (ref, index) for ref, count in zip(inner_refs, counts) for index in range(count)
        ]
        for expert, (ref, index) in enumerate(sources):
            place = pl.ds(expert * per, per)
            if expert < len(weights):
                weight = weight_refs[expert][...]
            else:
                moves[expert - len(weights)].wait()
                weight = late_ref[expert - len(weights)]
            out = jnp.dot(
                ref[pl.ds(index * per, per), :], weight, preferred_element_type=F32
            )
            out_ref[place, :] = (out * gate_ref[place, 0:1]).astype(BF16)
        for target, first in ((theirs_ref, half), (mine_ref, 0)):
            target[...] = jnp.dot(
                combine_ref[pl.ds(first, half), :], out_ref[...], preferred_element_type=F32
            ).astype(BF16)

    return call(
        kernel,
        "expert_down",
        2 * (max(1, len(late)) * depth + slots) * model + 3 * MIB,
        [VMEM, VMEM, ANY] + [VMEM] * (len(inners) + len(weights)),
        [pltpu.VMEM((half, model), BF16)] * 2,
        [
            combine,
            gates,
            pltpu.with_memory_space_constraint(array, pltpu.HBM),
            *inners,
            *[pltpu.with_memory_space_constraint(weight, pltpu.VMEM) for weight in weights],
        ],
        scratch=[
            pltpu.VMEM((max(1, len(late)), depth, model), BF16),
            pltpu.VMEM((slots, model), BF16),
            pltpu.SemaphoreType.DMA((max(1, len(late)),)),
        ],
        bytes_moved=2 * (len(weights) + len(late)) * depth * model,
        flops=2 * slots * model * depth,
    )


def add_pair(mine, theirs, count):
    total, width = mine.shape
    rows = total // count

    def kernel(mine_ref, theirs_ref, *outs):
        for index in range(count):
            place = pl.ds(index * rows, rows)
            outs[index][...] = (
                mine_ref[place, :].astype(F32) + theirs_ref[place, :].astype(F32)
            ).astype(BF16)

    return call(
        kernel,
        "add_pair",
        MIB,
        [VMEM] * 2,
        [jax.ShapeDtypeStruct((rows, width), BF16)] * count,
        [mine, theirs],
    )


def gather_sums(blocks, hidden, pieces):
    rows, model = hidden.shape
    count = len(blocks)
    width = model // pieces

    def kernel(*refs):
        parts = refs[:count]
        hidden_ref = refs[count]
        own_ref = refs[count + 1]
        sent = refs[count + 2 : -1]
        total_ref = refs[-1]
        mine = lax.axis_index("expert")
        total = parts[0][...].astype(F32)
        for part in parts[1:]:
            total = total + part[...].astype(F32)
        total_ref[...] = total
        for piece in range(pieces):
            columns = pl.ds(pl.multiple_of((mine ^ piece) * width, 128), width)
            if piece == 0:
                own_ref[...] = total_ref[:, columns] + hidden_ref[:, columns]
            else:
                sent[piece - 1][...] = total_ref[:, columns].astype(BF16)

    return call(
        kernel,
        "gather_sums",
        MIB,
        [VMEM] * (count + 1),
        [jax.ShapeDtypeStruct((rows, width), F32)]
        + [jax.ShapeDtypeStruct((rows, width), BF16)] * (pieces - 1),
        [*blocks, hidden],
        scratch=[pltpu.VMEM((rows, model), F32)],
    )


def body(
    layer_input,
    queries,
    new_keys,
    new_values,
    cache_keys,
    cache_values,
    parents,
    lengths,
    out_weight,
    norm_gain,
    expert_ids,
    gate_scores,
    up_weight,
    down_weight,
):
    beams = lax.axis_size("beam")
    zs = lax.axis_size("expert")
    chips = beams // 2
    spacing = beams // BEAM
    sents, past, width = cache_keys.shape
    rows = STEPS * sents
    model = layer_input.shape[2]
    local = up_weight.shape[0]

    held = local * HELD // 8
    loads = [(up_weight, expert) for expert in range(local)]
    loads += [(down_weight, expert) for expert in range(held)]
    cuts = [len(loads) * part // STAGES[-1] for part in STAGES]
    loads = [loads[low:high] for low, high in zip(cuts, cuts[1:])]
    weights = []

    message, entries, parents, lengths, norm_gain, ids, scores = pack(
        queries,
        new_keys,
        new_values,
        [
            layer_input,
            parents,
            lengths[None, :],
            norm_gain[None, :],
            expert_ids.transpose(0, 2, 1),
            gate_scores.transpose(0, 2, 1),
        ],
    )
    messages = [message] + [
        swapped(message, "beam", shift * spacing) for shift in range(1, BEAM)
    ]
    bias, select, route, place = masks(parents, lengths, ids, scores, past)
    (keys, values, weight, *some), done = bring(
        [
            (cache_keys.reshape(1, sents * past, width), None),
            (cache_values.reshape(1, sents * past, width), None),
            (out_weight[None], None),
        ]
        + loads[0],
        route,
    )
    weights += some
    chunks = attend(keys, values, messages, bias, route, [done])
    returned = exchanged(chunks, "beam", spacing)
    some, done = bring(loads[1], chunks[0])
    weights += some
    own, partial, routes = project(select, returned, weight, sents, [done])
    others = [swapped(partial, "expert", shift) for shift in range(1, zs)]
    if chips != BEAM or chunks[0].shape[0] == rows:
        routes = stack_rows(
            [route] + [swapped(route, "beam", 2 * shift) for shift in range(1, chips)], []
        )
    other_routes = swapped(routes, "beam", 1)
    some, done = bring(loads[2], partial)
    weights += some
    dispatch, combine, gates = routing(place, routes, other_routes, local, STEPS, sents, [done])
    hidden, column = normalize(entries, own, others, norm_gain, [dispatch])

    blocks = [column] + [swapped(column, "beam", 2 * shift) for shift in range(1, chips)]
    some, done = bring(loads[3], column)
    weights += some
    *blocks, done = lax.optimization_barrier((*blocks, done))
    blocks = blocks + [swapped(block, "beam", 1) for block in blocks]
    half = local // 2
    middle = range(held, min(held + MIDDLE, local))
    _, inner = expert_up(
        dispatch, blocks, weights[:half], 0, local, down_weight, [], done
    )
    some, other_inner = expert_up(
        dispatch, blocks, weights[half:local], half, local, down_weight, middle, inner
    )
    mine, theirs = expert_down(
        combine,
        gates,
        [inner, other_inner],
        weights[local:] + some,
        down_weight,
        range(middle.stop, local),
    )

    theirs = swapped(theirs, "beam", 1)
    sums = exchanged(add_pair(mine, theirs, chips), "beam", 2)
    cuts = gather_sums(sums, hidden, zs)
    mixed, *others = exchanged(cuts, "expert", 1)
    for part in others:
        mixed = mixed + part.astype(F32)
    return mixed.astype(BF16).reshape(STEPS, sents, width)


def solution(mesh):
    return jax.shard_map(
        body,
        mesh=mesh,
        in_specs=(
            P(None, "beam", None),
            P(None, "beam", "expert"),
            P(None, "beam", "expert"),
            P(None, "beam", "expert"),
            P("beam", None, "expert"),
            P("beam", None, "expert"),
            P(),
            P(),
            P("expert", None),
            P(),
            P(None, "beam", None),
            P(None, "beam", None),
            P("expert", None, "beam"),
            P("expert", "beam", None),
        ),
        out_specs=P(None, "beam", "expert"),
        check_vma=False,
    )
```

```python
import math

import jax
import jax.numpy as jnp
from jax import lax
from jax.experimental import pallas as pl
from jax.experimental.pallas import tpu as pltpu
from jax.sharding import PartitionSpec as P

HEAD_DIM = 128
TOP = 2
CAP = 2
BEAM = 4
STEPS = 2
HELD = 5
MIDDLE = 1
PARTS = 8
WIDE = 1024
NARROW = 512
STAGES = (0, 2, 5, 9, 13)
MIB = 1 << 20
BF16 = jnp.bfloat16
F32 = jnp.float32
ANY = pl.ANY
VMEM = pltpu.VMEM


def call(
    kernel, name, limit, in_spaces, outs, args, scratch=(), bytes_moved=MIB, flops=0, aliases=None
):
    return pl.pallas_call(
        kernel,
        name=name,
        out_shape=outs,
        in_specs=[pl.BlockSpec(memory_space=space) for space in in_spaces],
        out_specs=[pl.BlockSpec(memory_space=VMEM)] * len(outs),
        scratch_shapes=list(scratch),
        input_output_aliases=aliases or {},
        compiler_params=pltpu.CompilerParams(vmem_limit_bytes=limit),
        cost_estimate=pl.CostEstimate(flops=flops, bytes_accessed=bytes_moved, transcendentals=0),
    )(*args)


def swapped(value, axis, mask):
    count = lax.axis_size(axis)
    return lax.ppermute(value, axis, [(source, source ^ mask) for source in range(count)])


def exchanged(pieces, axis, unit):
    got = [swapped(pieces[index], axis, index * unit) for index in reversed(range(1, len(pieces)))]
    return [pieces[0]] + got[::-1]


def split_index(index, size):
    assert size & (size - 1) == 0
    return index >> (size.bit_length() - 1), index & (size - 1)


def here(sents):
    beam = lax.axis_index("beam")
    slot, rest = split_index(beam, lax.axis_size("beam") // BEAM)
    return slot, rest * sents


def iota(shape, dim):
    return lax.broadcasted_iota(jnp.int32, shape, dim)


def one_hot(condition):
    return jnp.where(condition, 1.0, 0.0).astype(BF16)


def pack(queries, new_keys, new_values, small):
    steps, sents, width = queries.shape
    parts = (queries, new_keys, new_values)
    count = len(parts)

    def kernel(*refs):
        sources = refs[: count + len(small)]
        out_ref = refs[count + len(small)]
        targets = refs[count + len(small) + 1 : -1]
        sem = refs[-1]
        copies = [
            (sources[place].at[step], out_ref.at[pl.ds((place * steps + step) * sents, sents)])
            for place in range(count)
            for step in range(steps)
        ]
        copies += list(zip(sources[count:], targets))
        copies = [
            pltpu.make_async_copy(source, target, sem.at[index])
            for index, (source, target) in enumerate(copies)
        ]
        for copy in copies:
            copy.start()
        for copy in copies:
            copy.wait()

    return call(
        kernel,
        "pack",
        MIB // 2,
        [ANY] * (count + len(small)),
        [pltpu.VMEM((count * steps * sents, width), BF16)]
        + [pltpu.VMEM(array.shape, array.dtype) for array in small],
        [pltpu.with_memory_space_constraint(part, pltpu.HBM) for part in (*parts, *small)],
        scratch=[pltpu.SemaphoreType.DMA((count * steps + len(small),))],
    )


def masks(parents, lengths, expert_ids, gate_scores, past):
    steps, _, sents = expert_ids.shape
    rows = steps * sents
    sent_total = lengths.shape[1]
    asked = BEAM * rows
    span = sents * past

    def kernel(*refs):
        parent_ref, length_ref, id_ref, gate_ref = refs[:4]
        bias_ref, select_ref, route_ref, place_ref = refs[4:]
        place_ref[...] = jnp.full((8, 128), lax.axis_index("expert"), jnp.int32)
        my_slot, first = here(sents)
        turn, rest = split_index(iota((asked, 1), 0), rows)
        step, rank = split_index(rest, sents)
        slot = my_slot ^ turn
        table = parent_ref[...].astype(F32).astype(BF16)
        contract = (((1,), (1,)), ((), ()))
        everyone = iota((asked, BEAM * sent_total), 1)
        source = one_hot(everyone == slot * sent_total + first + rank)
        found = lax.dot_general(source, table, contract, preferred_element_type=F32)
        before = found[:, 1:2].astype(jnp.int32)
        counts = length_ref[...].astype(F32).astype(BF16)
        sentence = one_hot(iota((asked, sent_total), 1) == first + rank)
        counts = jnp.broadcast_to(counts, (8, sent_total))
        valid = lax.dot_general(sentence, counts, contract, preferred_element_type=F32)
        valid = valid[:, 0:1].astype(jnp.int32)
        cached_sent, position = split_index(iota((asked, span), 1), past)
        bias_ref[:, pl.ds(0, span)] = jnp.where(
            (cached_sent == rank) & (position < valid), 0.0, -1e30
        )
        key_turn, key_rest = split_index(iota((asked, asked), 1), rows)
        key_step, key_rank = split_index(key_rest, sents)
        key_slot = my_slot ^ key_turn
        own = (key_turn == turn) & (key_step == step)
        earlier = (step == 1) & (key_step == 0) & (key_slot == before)
        bias_ref[:, pl.ds(span, asked)] = jnp.where(
            (key_rank == rank) & (own | earlier), 0.0, -1e30
        )
        chain = one_hot(
            everyone[:rows] == jnp.where(step[:rows] == 0, my_slot, before[:rows]) * sent_total
            + first
            + rank[:rows]
        )
        holder = lax.dot_general(chain, table, contract, preferred_element_type=F32)
        holder = holder[:, 0:1].astype(jnp.int32)
        holder = holder ^ my_slot
        select_ref[...] = one_hot(
            iota((rows, asked), 1) == holder * rows + iota((rows, asked), 0)
        )
        lane = iota((sents, 128), 1)
        square = iota((sents, sents), 0) == iota((sents, sents), 1)
        for step in range(steps):
            columns = []
            for part in (id_ref[step].astype(F32), gate_ref[step]):
                for choice in range(TOP):
                    line = jnp.where(square, part[choice : choice + 1, :], 0.0)
                    columns.append(jnp.sum(line, axis=1, keepdims=True))
            scores = columns[TOP:]
            share = [score / sum(scores) for score in scores]
            high = [part.astype(BF16).astype(F32) for part in share]
            columns[TOP:] = high + [part - top for part, top in zip(share, high)]
            route = jnp.zeros((sents, 128), F32)
            for index, column in enumerate(columns):
                route = jnp.where(lane == index, column, route)
            route_ref[pl.ds(step * sents, sents), :] = route.astype(BF16)

    return call(
        kernel,
        "masks",
        2 * MIB,
        [VMEM] * 4,
        [
            pltpu.VMEM((asked, span + asked), F32),
            pltpu.VMEM((rows, asked), BF16),
            pltpu.VMEM((rows, 128), BF16),
            pltpu.VMEM((8, 128), jnp.int32),
        ],
        [parents, lengths, expert_ids, gate_scores],
    )


def routing(place, mine, theirs, local, steps, sents, waits):
    total = 2 * mine.shape[0]
    rows = steps * sents
    beams = total // rows
    per = beams * steps * CAP
    slots = local * per
    step_rows = 128

    def kernel(*refs):
        place_ref, mine_ref, theirs_ref = refs[:3]
        dispatch_ref, combine_ref, gate_ref = refs[-3:]
        by_slot = jnp.zeros((slots, 1), F32)
        my_z = place_ref[0:1, 0:1]
        for start in range(0, total, step_rows):
            half, ref = divmod(start, total // 2)
            info = (theirs_ref if half else mine_ref)[pl.ds(ref, step_rows), :].astype(F32)
            turned = jnp.transpose(info)
            row = iota((step_rows, step_rows), 0)
            lane = iota((step_rows, step_rows), 1)
            earlier = (split_index(row, sents)[0] == split_index(lane, sents)[0]) & (lane < row)
            group = split_index(iota((step_rows, 1), 0) + start, sents)[0]
            columns = iota((step_rows, slots), 1)
            hits = []
            for choice in range(TOP):
                ids = info[:, choice : choice + 1]
                same = jnp.zeros((step_rows, step_rows), F32)
                for other in range(TOP):
                    same += jnp.where(earlier & (turned[other : other + 1, :] == ids), 1.0, 0.0)
                before = jnp.sum(same, axis=1, keepdims=True).astype(jnp.int32)
                slot = (ids.astype(jnp.int32) - my_z * local) * per + group * CAP + before
                hits.append(columns == slot)
            gates = jnp.zeros((step_rows, slots), F32)
            for choice in range(TOP):
                high, low = TOP + choice, 2 * TOP + choice
                share = info[:, high : high + 1] + info[:, low : low + 1]
                gates = jnp.where(hits[choice], share, gates)
            by_slot += jnp.sum(jnp.transpose(gates), axis=1, keepdims=True)
            natural = one_hot(hits[0] | hits[1])
            combine_ref[pl.ds(start, step_rows), :] = natural
            dispatch_ref[:, pl.ds(start, step_rows)] = jnp.transpose(
                natural.astype(F32)
            ).astype(BF16)
        gate_ref[...] = jnp.broadcast_to(by_slot, (slots, 128))

    return call(
        kernel,
        "routing",
        max(2, total // 128) * MIB,
        [VMEM, VMEM, VMEM] + [ANY] * len(waits),
        [
            jax.ShapeDtypeStruct((slots, total), BF16),
            jax.ShapeDtypeStruct((total, slots), BF16),
            jax.ShapeDtypeStruct((slots, 128), F32),
        ],
        [place, mine, theirs, *waits],
    )


def stack_rows(parts, waits):
    rows, width = parts[0].shape

    def kernel(*refs):
        for index in range(len(parts)):
            refs[-1][pl.ds(index * rows, rows), :] = refs[index][...]

    return call(
        kernel,
        "stack_rows",
        MIB,
        [VMEM] * len(parts) + [ANY] * len(waits),
        [jax.ShapeDtypeStruct((len(parts) * rows, width), parts[0].dtype)],
        [*parts, *waits],
    )[0]


def start_parts(source, target, sem):
    rows = source.shape[0] // PARTS
    for part in range(PARTS):
        place = pl.ds(part * rows, rows)
        pltpu.make_async_copy(source.at[place], target.at[place], sem).start()


def bring(pieces, after):
    count = len(pieces)
    shapes = [array.shape if index is None else array.shape[1:] for array, index in pieces]

    def kernel(*refs):
        targets = refs[count + 1 : 2 * count + 1]
        done_ref, sem = refs[-2:]
        moves = []
        for place, (_, index) in enumerate(pieces):
            source = refs[place] if index is None else refs[place].at[index]
            moves.append(pltpu.make_async_copy(source, targets[place], sem.at[place]))
        for move in moves:
            move.start()
        done_ref[...] = jnp.zeros_like(done_ref)
        for move in moves:
            move.wait()

    *brought, done = call(
        kernel,
        "bring",
        MIB // 2,
        [ANY] * (count + 1),
        [pltpu.VMEM(shape, array.dtype) for shape, (array, _) in zip(shapes, pieces)]
        + [jax.ShapeDtypeStruct((8, 128), F32)],
        [pltpu.with_memory_space_constraint(array, pltpu.HBM) for array, _ in pieces] + [after],
        scratch=[pltpu.SemaphoreType.DMA((max(1, count),))],
        bytes_moved=4 * sum(math.prod(shape) for shape in shapes),
    )
    return brought, done


def attend(keys, values, messages, bias, route, waits):
    count = len(messages)
    rows = route.shape[0]
    steps, sents = STEPS, rows // STEPS
    width = messages[0].shape[1]
    heads = width // HEAD_DIM
    total = count * rows
    past = keys.shape[1]
    routed = sents if width >= steps * 128 else 0

    def kernel(*refs):
        key_ref, value_ref, bias_ref, route_ref = refs[:4]
        parts = refs[4 : 4 + count]
        outs = refs[4 + count + len(waits) : 4 + 2 * count + len(waits)]
        q_ref, k_ref, v_ref = refs[-3:]
        for index, part in enumerate(parts):
            place = pl.ds(index * rows, rows)
            q_ref[place, :] = part[pl.ds(0, rows), :]
            k_ref[place, :] = part[pl.ds(rows, rows), :]
            v_ref[place, :] = part[pl.ds(2 * rows, rows), :]
        if routed:
            for out in outs:
                out[pl.ds(rows, sents), :] = jnp.zeros((sents, width), BF16)
                for step in range(steps):
                    out[pl.ds(rows, sents), pl.ds(step * 128, 128)] = route_ref[
                        pl.ds(step * sents, sents), :
                    ]
        contract = (((1,), (1,)), ((), ()))
        for head in range(heads):
            cols = pl.ds(head * HEAD_DIM, HEAD_DIM)
            query = q_ref[:, cols]
            old = lax.dot_general(query, key_ref[0, :, cols], contract, preferred_element_type=F32)
            new = lax.dot_general(query, k_ref[:, cols], contract, preferred_element_type=F32)
            old = old * HEAD_DIM ** (-0.5) + bias_ref[:, pl.ds(0, past)]
            new = new * HEAD_DIM ** (-0.5) + bias_ref[:, pl.ds(past, total)]
            top = jnp.maximum(
                jnp.max(old, axis=-1, keepdims=True), jnp.max(new, axis=-1, keepdims=True)
            )
            old = jnp.exp(old - top)
            new = jnp.exp(new - top)
            norm = jnp.sum(old, axis=-1, keepdims=True) + jnp.sum(new, axis=-1, keepdims=True)
            old = (old / norm).astype(BF16)
            new = (new / norm).astype(BF16)
            out = jnp.dot(old, value_ref[0, :, cols], preferred_element_type=F32) + jnp.dot(
                new, v_ref[:, cols], preferred_element_type=F32
            )
            out = out.astype(BF16)
            for index in range(count):
                outs[index][pl.ds(0, rows), cols] = out[index * rows : (index + 1) * rows, :]

    return call(
        kernel,
        "attend",
        2 * MIB,
        [VMEM] * (4 + count) + [ANY] * len(waits),
        [jax.ShapeDtypeStruct((rows + routed, width), BF16)] * count,
        [keys, values, bias, route, *messages, *waits],
        scratch=[pltpu.VMEM((total, width), BF16)] * 3,
    )


def project(select, chunks, weight, sents, waits):
    count = len(chunks)
    width = chunks[0].shape[1]
    rows = select.shape[0]
    steps = rows // sents
    model = weight.shape[2]
    routed = chunks[0].shape[0] > rows

    def kernel(*refs):
        select_ref, weight_ref = refs[:2]
        parts = refs[2 : 2 + count]
        own_ref, sent_ref, route_ref, all_ref = refs[-4:]
        for index in range(count):
            all_ref[pl.ds(index * rows, rows), :] = parts[index][pl.ds(0, rows), :]
        picked = jnp.dot(select_ref[...], all_ref[...], preferred_element_type=F32).astype(BF16)
        product = jnp.dot(picked, weight_ref[0], preferred_element_type=F32)
        own_ref[...] = product
        sent_ref[...] = product.astype(BF16)
        for index in range(count):
            for step in range(steps):
                place = pl.ds(index * rows + step * sents, sents)
                if routed:
                    route_ref[place, :] = parts[index][pl.ds(rows, sents), pl.ds(step * 128, 128)]
                else:
                    route_ref[place, :] = jnp.zeros((sents, 128), BF16)

    return call(
        kernel,
        "project",
        2 * MIB,
        [VMEM] * (2 + count) + [ANY] * len(waits),
        [
            jax.ShapeDtypeStruct((rows, model), F32),
            jax.ShapeDtypeStruct((rows, model), BF16),
            jax.ShapeDtypeStruct((count * rows, 128), BF16),
        ],
        [select, weight, *chunks, *waits],
        scratch=[pltpu.VMEM((count * rows, width), BF16)],
    )


def normalize(entry, own, others, gain, waits):
    rows, model = own.shape
    steps, sents, _ = entry.shape

    def kernel(*refs):
        entry_ref, gain_ref, own_ref = refs[:3]
        parts = refs[3 : 3 + len(others)]
        hidden_ref, normed_ref = refs[-2:]
        for step in range(steps):
            place = pl.ds(step * sents, sents)
            hidden = own_ref[place, :]
            for part in parts:
                hidden = hidden + part[place, :].astype(F32)
            hidden = entry_ref[step].astype(F32) + hidden
            center = hidden - jnp.mean(hidden, axis=-1, keepdims=True)
            spread = jnp.mean(center * center, axis=-1, keepdims=True)
            hidden_ref[place, :] = hidden
            normed_ref[place, :] = (center * lax.rsqrt(spread + 1e-05) * gain_ref[...]).astype(
                BF16
            )

    return call(
        kernel,
        "normalize",
        MIB,
        [VMEM] * (3 + len(others)) + [ANY] * len(waits),
        [jax.ShapeDtypeStruct((rows, model), F32), jax.ShapeDtypeStruct((rows, model), BF16)],
        [entry, gain, own, *others, *waits],
    )


def expert_up(dispatch, blocks, weights, first, local, array, later, after):
    per = dispatch.shape[0] // local
    total = dispatch.shape[1]
    rows, model = blocks[0].shape
    count = len(blocks)
    width = weights[0].shape[1]
    slots = per * len(weights)
    late = len(later)

    def kernel(*refs):
        dispatch_ref, later_ref = refs[:2]
        parts = refs[2 : 2 + count]
        weight_refs = refs[2 + count : 2 + count + len(weights)]
        targets = refs[3 + count + len(weights) : 3 + count + len(weights) + late]
        out_ref, all_ref, sorted_ref, sem = refs[-4:]
        moves = [
            pltpu.make_async_copy(later_ref.at[index], targets[place], sem.at[place])
            for place, index in enumerate(later)
        ]
        for place, index in enumerate(later):
            start_parts(later_ref.at[index], targets[place], sem.at[place])
        for index in range(count):
            all_ref[pl.ds(index * rows, rows), :] = parts[index][...]
        for start in range(0, model, NARROW):
            columns = pl.ds(start, NARROW)
            sorted_ref[:, columns] = jnp.dot(
                dispatch_ref[pl.ds(first * per, slots), :],
                all_ref[:, columns],
                preferred_element_type=F32,
            ).astype(BF16)
        for expert, weight_ref in enumerate(weight_refs):
            place = pl.ds(expert * per, per)
            inner = jnp.dot(sorted_ref[place, :], weight_ref[...], preferred_element_type=F32)
            out_ref[place, :] = jnp.maximum(inner, 0.0).astype(BF16)
        for move in moves:
            move.wait()

    *brought, inner = call(
        kernel,
        "expert_up",
        2 * (total + slots) * model + MIB,
        [VMEM, ANY] + [VMEM] * (count + len(weights)) + [ANY],
        [pltpu.VMEM(array.shape[1:], BF16)] * late + [pltpu.VMEM((slots, width), BF16)],
        [
            dispatch,
            pltpu.with_memory_space_constraint(array, pltpu.HBM),
            *blocks,
            *[pltpu.with_memory_space_constraint(weight, pltpu.VMEM) for weight in weights],
            after,
        ],
        scratch=[
            pltpu.VMEM((total, model), BF16),
            pltpu.VMEM((slots, model), BF16),
            pltpu.SemaphoreType.DMA((max(1, late),)),
        ],
        bytes_moved=2 * len(weights) * model * width,
        flops=2 * slots * model * width,
    )
    return brought, inner


def expert_down(combine, gates, inners, weights, array, late):
    rows, slots = combine.shape
    depth, model = array.shape[1:]
    per = slots // (len(weights) + len(late))
    half = rows // 2
    counts = [inner.shape[0] // per for inner in inners]

    def kernel(*refs):
        combine_ref, gate_ref, array_ref = refs[:3]
        inner_refs = refs[3 : 3 + len(inners)]
        weight_refs = refs[3 + len(inners) : 3 + len(inners) + len(weights)]
        mine_ref, theirs_ref, late_ref, out_ref, sem = refs[-5:]
        moves = [
            pltpu.make_async_copy(array_ref.at[index], late_ref.at[place], sem.at[place])
            for place, index in enumerate(late)
        ]
        for place, index in enumerate(late):
            start_parts(array_ref.at[index], late_ref.at[place], sem.at[place])
        sources = [
            (ref, index) for ref, count in zip(inner_refs, counts) for index in range(count)
        ]
        for expert, (ref, index) in enumerate(sources):
            place = pl.ds(expert * per, per)
            if expert < len(weights):
                weight = weight_refs[expert]
            else:
                moves[expert - len(weights)].wait()
                weight = late_ref.at[expert - len(weights)]
            for start in range(0, model, WIDE):
                columns = pl.ds(start, WIDE)
                out = jnp.dot(
                    ref[pl.ds(index * per, per), :],
                    weight[:, columns],
                    preferred_element_type=F32,
                )
                out_ref[place, columns] = (out * gate_ref[place, 0:1]).astype(BF16)
        for target, first in ((theirs_ref, half), (mine_ref, 0)):
            for start in range(0, model, NARROW):
                columns = pl.ds(start, NARROW)
                target[:, columns] = jnp.dot(
                    combine_ref[pl.ds(first, half), :],
                    out_ref[:, columns],
                    preferred_element_type=F32,
                ).astype(BF16)

    return call(
        kernel,
        "expert_down",
        2 * (max(1, len(late)) * depth + slots) * model + 3 * MIB,
        [VMEM, VMEM, ANY] + [VMEM] * (len(inners) + len(weights)),
        [pltpu.VMEM((half, model), BF16)] * 2,
        [
            combine,
            gates,
            pltpu.with_memory_space_constraint(array, pltpu.HBM),
            *inners,
            *[pltpu.with_memory_space_constraint(weight, pltpu.VMEM) for weight in weights],
        ],
        scratch=[
            pltpu.VMEM((max(1, len(late)), depth, model), BF16),
            pltpu.VMEM((slots, model), BF16),
            pltpu.SemaphoreType.DMA((max(1, len(late)),)),
        ],
        bytes_moved=2 * (len(weights) + len(late)) * depth * model,
        flops=2 * slots * model * depth,
    )


def add_pair(mine, theirs, count):
    total, width = mine.shape
    rows = total // count

    def kernel(mine_ref, theirs_ref, *outs):
        for index in range(count):
            place = pl.ds(index * rows, rows)
            outs[index][...] = (
                mine_ref[place, :].astype(F32) + theirs_ref[place, :].astype(F32)
            ).astype(BF16)

    return call(
        kernel,
        "add_pair",
        MIB,
        [VMEM] * 2,
        [jax.ShapeDtypeStruct((rows, width), BF16)] * count,
        [mine, theirs],
    )


def gather_sums(blocks, hidden, pieces):
    rows, model = hidden.shape
    count = len(blocks)
    width = model // pieces

    def kernel(*refs):
        parts = refs[:count]
        hidden_ref = refs[count]
        own_ref = refs[count + 1]
        sent = refs[count + 2 : -1]
        total_ref = refs[-1]
        mine = lax.axis_index("expert")
        total = parts[0][...].astype(F32)
        for part in parts[1:]:
            total = total + part[...].astype(F32)
        total_ref[...] = total
        for piece in range(pieces):
            columns = pl.ds(pl.multiple_of((mine ^ piece) * width, 128), width)
            if piece == 0:
                own_ref[...] = total_ref[:, columns] + hidden_ref[:, columns]
            else:
                sent[piece - 1][...] = total_ref[:, columns].astype(BF16)

    return call(
        kernel,
        "gather_sums",
        MIB,
        [VMEM] * (count + 1),
        [jax.ShapeDtypeStruct((rows, width), F32)]
        + [jax.ShapeDtypeStruct((rows, width), BF16)] * (pieces - 1),
        [*blocks, hidden],
        scratch=[pltpu.VMEM((rows, model), F32)],
    )


def body(
    layer_input,
    queries,
    new_keys,
    new_values,
    cache_keys,
    cache_values,
    parents,
    lengths,
    out_weight,
    norm_gain,
    expert_ids,
    gate_scores,
    up_weight,
    down_weight,
):
    beams = lax.axis_size("beam")
    zs = lax.axis_size("expert")
    chips = beams // 2
    spacing = beams // BEAM
    sents, past, width = cache_keys.shape
    rows = STEPS * sents
    model = layer_input.shape[2]
    local = up_weight.shape[0]

    held = local * HELD // 8
    loads = [(up_weight, expert) for expert in range(local)]
    loads += [(down_weight, expert) for expert in range(held)]
    cuts = [len(loads) * part // STAGES[-1] for part in STAGES]
    loads = [loads[low:high] for low, high in zip(cuts, cuts[1:])]
    weights = []

    message, entries, parents, lengths, norm_gain, ids, scores = pack(
        queries,
        new_keys,
        new_values,
        [
            layer_input,
            parents,
            lengths[None, :],
            norm_gain[None, :],
            expert_ids.transpose(0, 2, 1),
            gate_scores.transpose(0, 2, 1),
        ],
    )
    messages = [message] + [
        swapped(message, "beam", shift * spacing) for shift in range(1, BEAM)
    ]
    bias, select, route, place = masks(parents, lengths, ids, scores, past)
    (keys, values, weight, *some), done = bring(
        [
            (cache_keys.reshape(1, sents * past, width), None),
            (cache_values.reshape(1, sents * past, width), None),
            (out_weight[None], None),
        ]
        + loads[0],
        route,
    )
    weights += some
    chunks = attend(keys, values, messages, bias, route, [done])
    returned = exchanged(chunks, "beam", spacing)
    some, done = bring(loads[1], chunks[0])
    weights += some
    own, partial, routes = project(select, returned, weight, sents, [done])
    others = [swapped(partial, "expert", shift) for shift in range(1, zs)]
    if chips != BEAM or chunks[0].shape[0] == rows:
        routes = stack_rows(
            [route] + [swapped(route, "beam", 2 * shift) for shift in range(1, chips)], []
        )
    other_routes = swapped(routes, "beam", 1)
    some, done = bring(loads[2], partial)
    weights += some
    dispatch, combine, gates = routing(place, routes, other_routes, local, STEPS, sents, [done])
    hidden, column = normalize(entries, own, others, norm_gain, [dispatch])

    blocks = [column] + [swapped(column, "beam", 2 * shift) for shift in range(1, chips)]
    some, done = bring(loads[3], column)
    weights += some
    *blocks, done = lax.optimization_barrier((*blocks, done))
    blocks = blocks + [swapped(block, "beam", 1) for block in blocks]
    half = local // 2
    middle = range(held, min(held + MIDDLE, local))
    _, inner = expert_up(
        dispatch, blocks, weights[:half], 0, local, down_weight, [], done
    )
    some, other_inner = expert_up(
        dispatch, blocks, weights[half:local], half, local, down_weight, middle, inner
    )
    mine, theirs = expert_down(
        combine,
        gates,
        [inner, other_inner],
        weights[local:] + some,
        down_weight,
        range(middle.stop, local),
    )

    theirs = swapped(theirs, "beam", 1)
    sums = exchanged(add_pair(mine, theirs, chips), "beam", 2)
    cuts = gather_sums(sums, hidden, zs)
    mixed, *others = exchanged(cuts, "expert", 1)
    for part in others:
        mixed = mixed + part.astype(F32)
    return mixed.astype(BF16).reshape(STEPS, sents, width)


def solution(mesh):
    return jax.shard_map(
        body,
        mesh=mesh,
        in_specs=(
            P(None, "beam", None),
            P(None, "beam", "expert"),
            P(None, "beam", "expert"),
            P(None, "beam", "expert"),
            P("beam", None, "expert"),
            P("beam", None, "expert"),
            P(),
            P(),
            P("expert", None),
            P(),
            P(None, "beam", None),
            P(None, "beam", None),
            P("expert", None, "beam"),
            P("expert", "beam", None),
        ),
        out_specs=P(None, "beam", "expert"),
        check_vma=False,
    )
```
